768 devices in a mesh: blk: 32 (over z_hi, y, core), group: 24 (over x, z_lo).
Axes of the slice: x: 4, y: 8, z: 12 (z_hi: 2, z_lo: 6; z = z_hi * 6 + z_lo), core: 2. Of those that a mesh axis runs over, the one named last changes fastest.
Arguments:
- image_embed: float32 [196608, 1152], P(('blk', 'group')), may hold values from -2.5 to 2.5
- text_embed: float32 [196608, 1152], P(('blk', 'group')), may hold values from -2.5 to 2.5
- logit_scale: float32 [1], replicated, may hold values from 2 to 8
- logit_bias: float32 [1], replicated, may hold values from -3 to -0.5
Outputs:
- picture_vector_derivative: float32 [196608, 1152], P(('blk', 'group'))
- caption_vector_derivative: float32 [196608, 1152], P(('blk', 'group'))
- logit_scaling_derivative: float32 [1], replicated
The draws below stay inside these ranges and needn't reach their ends.
All inputs are finite; a program needn't handle non-finite values.
Results may differ from the reference program's by a relative error of at most 0.0065.
Values may be sent and summed in bfloat16 or wider, within the bound.
A program may use at most 32 MiB of HBM per device.

```python
import math
import jax
import jax.numpy as jnp
from jax import lax

D = 1152
ROWS = 256
HALF = 2
MATCHED_SAMPLES = 196608
N_BLK = 32
N_GROUP = 24


def shared_parts(key):
    base = jnp.clip(jax.random.normal(jax.random.fold_in(key, 1), (MATCHED_SAMPLES, D), jnp.float32), -4.5, 4.5)
    direction = jnp.clip(jax.random.normal(jax.random.fold_in(key, 2), (1, D), jnp.float32), -4.5, 4.5)
    group_level = jax.random.uniform(jax.random.fold_in(key, 3), (N_GROUP,), jnp.float32, 0.02, 0.08)
    block_level = jax.random.uniform(jax.random.fold_in(key, 4), (N_BLK,), jnp.float32, 0.5, 1.5)
    jitter = jax.random.uniform(jax.random.fold_in(key, 5), (N_BLK, N_GROUP), jnp.float32, 0.8, 1.2)
    block_align = jax.random.uniform(jax.random.fold_in(key, 6), (N_BLK, N_GROUP), jnp.float32, 0.2, 0.9)
    row_jitter = jax.random.uniform(jax.random.fold_in(key, 8), (MATCHED_SAMPLES,), jnp.float32, -0.05, 0.05)
    index = jnp.arange(MATCHED_SAMPLES, dtype=jnp.int32)
    place = index // (ROWS * N_GROUP)
    cycle = index // ROWS % N_GROUP
    share = (block_level[place] * group_level[cycle] * jitter[place, cycle])[:, None]
    align = (block_align[place, cycle] + row_jitter)[:, None]
    return (base, direction, share, align)


def draw_image_embed(key, part):
    base, direction, share, align = shared_parts(key)
    mixed = jnp.sqrt(1.0 - share * share) * base + share * direction
    return 0.03 * mixed


def draw_text_embed(key, part):
    base, direction, share, align = shared_parts(key)
    key = jax.random.fold_in(key, 13)
    noise = jnp.clip(jax.random.normal(key, (MATCHED_SAMPLES, D), jnp.float32), -4.5, 4.5)
    own = align * base + jnp.sqrt(1.0 - align * align) * noise
    mixed = jnp.sqrt(1.0 - share * share) * own + share * direction
    return 0.03 * mixed


def setup_inputs(seed: int = 0) -> dict:
    splits = jax.random.split(jax.random.key(seed), 5)
    image_embed = draw_image_embed(jax.random.fold_in(splits[4], 71), 0)
    text_embed = draw_text_embed(jax.random.fold_in(splits[4], 71), 0)
    logit_scale = jnp.clip(jnp.exp(jax.random.uniform(splits[2], (1,), jnp.float32, math.log(2.0), math.log(8.0))), 2.0, 8.0)
    logit_bias = jnp.clip(jax.random.uniform(splits[3], (1,), jnp.float32, -3.0, -0.5), -3.0, -0.5)
    return {"image_embed": image_embed, "text_embed": text_embed, "logit_scale": logit_scale, "logit_bias": logit_bias}


def reference(image_embed, text_embed, logit_scale, logit_bias):
    temper = logit_scale[0]
    offset = logit_bias[0]
    image_inv = lax.rsqrt(lax.optimization_barrier(jnp.sum(image_embed * image_embed, axis=1, keepdims=True)) + 1e-06)
    text_inv = lax.rsqrt(lax.optimization_barrier(jnp.sum(text_embed * text_embed, axis=1, keepdims=True)) + 1e-06)
    image_unit = image_embed * image_inv
    text_unit = text_embed * text_inv
    image_low = image_unit.astype(jnp.bfloat16)
    text_low = text_unit.astype(jnp.bfloat16)
    images = jnp.swapaxes(image_low.reshape(N_BLK, N_GROUP, ROWS, D), 0, 1)
    texts = jnp.swapaxes(text_low.reshape(N_BLK, N_GROUP, ROWS, D), 0, 1)
    identity = jnp.eye(ROWS, dtype=jnp.float32)
    highest = lax.Precision.HIGHEST

    def one_cycle(pair):
        image_block, text_block = pair
        image_wide = image_block.astype(jnp.float32)
        image_dir = jnp.zeros((N_BLK, ROWS, D), jnp.float32)
        text_dir = jnp.zeros((N_BLK, ROWS, D), jnp.float32)
        scale_total = jnp.zeros((), jnp.float32)
        for offset_k in range(-HALF, HALF + 1):
            moved = jnp.roll(text_block, -offset_k, axis=0).astype(jnp.float32)
            inner = jnp.einsum('brd,bsd->brs', image_wide, moved, precision=highest)
            logits = temper * inner + offset
            if offset_k == 0:
                sign = 2.0 * identity - 1.0
            else:
                sign = -jnp.ones((ROWS, ROWS), jnp.float32)
            coeff = (-sign * jax.nn.sigmoid(-sign * logits)).astype(jnp.bfloat16).astype(jnp.float32)
            image_dir = image_dir + temper * jnp.einsum('brs,bsd->brd', coeff, moved, precision=highest)
            term = temper * jnp.einsum('brs,brd->bsd', coeff, image_wide, precision=highest)
            text_dir = text_dir + jnp.roll(term, offset_k, axis=0)
            scale_total = scale_total + jnp.sum(coeff * inner)
        return (image_dir, text_dir, scale_total)
    image_dirs, text_dirs, cumulative_partial_sums = lax.map(one_cycle, (images, texts))
    image_dir = jnp.swapaxes(image_dirs, 0, 1).reshape(N_BLK * N_GROUP * ROWS, D)
    text_dir = jnp.swapaxes(text_dirs, 0, 1).reshape(N_BLK * N_GROUP * ROWS, D)
    picture_vector_derivative = image_inv * (image_dir - image_unit * lax.optimization_barrier(jnp.sum(image_unit * image_dir, axis=1, keepdims=True)))
    caption_vector_derivative = text_inv * (text_dir - text_unit * lax.optimization_barrier(jnp.sum(text_unit * text_dir, axis=1, keepdims=True)))
    logit_scaling_derivative = jnp.reshape(jnp.sum(cumulative_partial_sums) / MATCHED_SAMPLES, (1,))
    return (picture_vector_derivative, caption_vector_derivative, logit_scaling_derivative)
```

```python
import functools

import jax
import jax.numpy as jnp
from jax import lax
from jax.experimental import pallas as pl
from jax.experimental.pallas import tpu as pltpu
from jax.sharding import PartitionSpec as P

MESH = pl.DeviceIdType.MESH

NY, NX, ZH, ZL = 8, 4, 2, 6
NZ = ZH * ZL

UP, DN, SIB, FWD, RELAY, OWN = range(6)
IMG, TXT = 0, 1

CHUNKS = 4
DIRECT = 2
STRIP = 32


def kernel(
    scale_ref, bias_ref, image_hbm, text_hbm, image_out, text_out, scale_out,
    feat, raw, inv, acc, part, red_c, red_y, red_z, red_x,
    load_sem, out_sem, send_sem, fwd_sem, relay_sem, recv_sem, red_send, red_recv,
):
    rows, width = image_hbm.shape
    step = rows // CHUNKS
    b, g = lax.axis_index("blk"), lax.axis_index("group")
    zh, y, c = b // (2 * NY), (b // 2) % NY, b % 2
    x, zl = g // ZL, g % ZL
    z = zh * ZL + zl

    def dev(x, y, z, c):
        return ((z // ZL) * (2 * NY) + y * 2 + c, x * ZL + z % ZL)

    other_core = dev(x, y, z, 1 - c)
    far_z = (z + ZL) % NZ

    barrier = pltpu.get_barrier_semaphore()
    peers = [other_core]
    peers += [dev(x, (y + d) % NY, z, c) for d in range(1, NY)]
    peers += [dev(x, y, (z + d) % NZ, c) for d in range(1, NZ)]
    peers += [dev((x + d) % NX, y, z, c) for d in range(1, NX)]
    peers += [dev(x, (y + d) % NY, far_z, c) for d in (1, 2, NY - 1, NY - 2)]
    for peer in peers:
        pl.semaphore_signal(barrier, inc=1, device_id=peer, device_id_type=MESH)

    loads = [
        pltpu.make_async_copy(image_hbm, raw.at[IMG], load_sem.at[IMG]),
        pltpu.make_async_copy(text_hbm, raw.at[TXT], load_sem.at[TXT]),
    ]
    loads[TXT].start()
    loads[IMG].start()

    def normalize(kind):
        def strip(i, carry):
            at = pl.ds(pl.multiple_of(i * STRIP, STRIP), STRIP)
            value = raw[kind, at, :]
            scale = lax.rsqrt(jnp.sum(value * value, axis=1, keepdims=True) + 1e-06)
            inv[kind, at, :] = jnp.broadcast_to(scale, (STRIP, 128))
            feat[OWN, kind, at, :] = (value * scale).astype(jnp.bfloat16)
            return carry

        lax.fori_loop(0, rows // STRIP, strip, 0)

    def remote(src_slot, dst_slot, kind, j, send, device):
        at = pl.ds(pl.multiple_of(j * step, step), step)
        return pltpu.make_async_remote_copy(
            src_ref=feat.at[src_slot, kind, at],
            dst_ref=feat.at[dst_slot, kind, at],
            send_sem=send,
            recv_sem=recv_sem.at[dst_slot, kind, j],
            device_id=device,
            device_id_type=MESH,
        )

    def pick(cond, a, b):
        return jnp.where(cond, a, b)

    def own_sends(kind, j):
        relayed = j >= DIRECT
        seam = y == NY - 1
        hop = seam & relayed
        up_y = pick(hop, y - 1, (y + 1) % NY)
        up_z = pick(seam & jnp.logical_not(relayed), far_z, z)
        up_slot = pick(hop, RELAY, DN)
        up = remote(OWN, up_slot, kind, j, send_sem.at[0, kind, j], dev(x, up_y, up_z, c))
        seam = y == 0
        hop = seam & relayed
        dn_y = pick(hop, y + 1, (y + NY - 1) % NY)
        dn_z = pick(seam & jnp.logical_not(relayed), far_z, z)
        dn_slot = pick(hop, RELAY, UP)
        down = remote(OWN, dn_slot, kind, j, send_sem.at[1, kind, j], dev(x, dn_y, dn_z, c))
        side = remote(OWN, SIB, kind, j, send_sem.at[2, kind, j], other_core)
        return up, down, side

    def send_own(kind):
        def one(i, carry):
            j = (i + DIRECT) % CHUNKS
            for copy in own_sends(kind, j):
                copy.start()
            return carry

        lax.fori_loop(0, CHUNKS, one, 0)

    def relay_copy(kind, j):
        to_y = pick(y == NY - 2, 0, NY - 1)
        slot = pick(y == NY - 2, DN, UP)
        return remote(RELAY, slot, kind, j, relay_sem.at[kind, j], dev(x, to_y, far_z, c))

    is_relay = (y == NY - 2) | (y == 1)

    def arrived(slot, kind, j):
        remote(OWN, slot, kind, j, fwd_sem.at[kind, j], other_core).wait_recv()

    from_slot = pick(c == 0, UP, DN)
    rest_slot = pick(c == 0, DN, UP)

    def pass_on(kind):
        def one(i, carry):
            j = (i + DIRECT) % CHUNKS if False else i
            arrived(from_slot, kind, j)
            remote(from_slot, FWD, kind, j, fwd_sem.at[kind, j], other_core).start()
            return carry

        lax.fori_loop(0, CHUNKS, one, 0)

    def await_block(slot, kind):
        def one(j, carry):
            arrived(slot, kind, j)
            return carry

        lax.fori_loop(0, CHUNKS, one, 0)

    temper = scale_ref[0]
    offset = bias_ref[0]

    def pair(slot, kind, own):
        mine = 1 - kind
        inner = lax.dot_general(
            feat[OWN, mine], feat[slot, kind], (((1,), (1,)), ((), ())),
            preferred_element_type=jnp.float32,
        )
        logits = temper * inner + offset
        if own:
            r = lax.broadcasted_iota(jnp.int32, (rows, rows), 0)
            s = lax.broadcasted_iota(jnp.int32, (rows, rows), 1)
            sign = jnp.where(r == s, 1.0, -1.0)
            coeff = -sign / (1.0 + jnp.exp(sign * logits))
        else:
            coeff = 1.0 / (1.0 + jnp.exp(-logits))
        coeff = coeff.astype(jnp.bfloat16)
        term = jnp.dot(coeff, feat[slot, kind], preferred_element_type=jnp.float32)
        if own:
            acc[mine] = term
        else:
            acc[mine] += term
        if kind == TXT:
            share = coeff.astype(jnp.float32) * inner
            share = jnp.sum(share.reshape(rows // 8, 8, rows), axis=0)
            share = share[:, :128] + share[:, 128:]
            if own:
                part[...] = share
            else:
                part[...] += share

    def finish(kind):
        out = (image_out, text_out)[kind]

        def strip(i, carry):
            at = pl.ds(pl.multiple_of(i * STRIP, STRIP), STRIP)
            scale = inv[kind, at, :][:, :1]
            unit = raw[kind, at, :] * scale
            direction = temper * acc[kind, at, :]
            along = jnp.sum(unit * direction, axis=1, keepdims=True)
            acc[kind, at, :] = scale * (direction - unit * along)
            return carry

        lax.fori_loop(0, rows // STRIP, strip, 0)
        pltpu.make_async_copy(acc.at[kind], out, out_sem.at[kind]).start()

    def reduce_over(buf, n, me, at, base):
        buf[me] = part[...]
        copies = []
        for d in range(1, n):
            copy = pltpu.make_async_remote_copy(
                src_ref=part,
                dst_ref=buf.at[me],
                send_sem=red_send.at[base + d - 1],
                recv_sem=red_recv.at[base + d - 1],
                device_id=at((me + d) % n),
                device_id_type=MESH,
            )
            copy.start()
            copies.append(copy)
        for copy in copies:
            copy.wait()
        total = buf[0]
        for i in range(1, n):
            total = total + buf[i]
        part[...] = total
        return base + n - 1

    loads[TXT].wait()
    normalize(TXT)
    pl.semaphore_wait(barrier, len(peers))
    send_own(TXT)
    loads[IMG].wait()
    normalize(IMG)
    send_own(IMG)

    @pl.when(is_relay)
    def _():
        for kind in (TXT, IMG):
            for j in range(DIRECT, CHUNKS):
                arrived(RELAY, kind, j)
                relay_copy(kind, j).start()

    pair(OWN, TXT, True)
    pair(OWN, IMG, True)

    def others(kind):
        await_block(SIB, kind)
        pair(SIB, kind, False)
        pass_on(kind)
        pair(from_slot, kind, False)

        def one(i, carry):
            slot = pick(i == 0, rest_slot, FWD)
            await_block(slot, kind)
            pair(slot, kind, False)
            return carry

        lax.fori_loop(0, 2, one, 0)

    others(TXT)
    finish(IMG)
    base = reduce_over(red_c, 2, c, lambda i: dev(x, y, z, i), 0)
    base = reduce_over(red_y, NY, y, lambda i: dev(x, i, z, c), base)
    base = reduce_over(red_x, NX, x, lambda i: dev(i, y, z, c), base)
    base = reduce_over(red_z, NZ, z, lambda i: dev(x, y, i, c), base)
    scale_out[0] = jnp.sum(part[...]) / (rows * NX * NY * NZ * 2)
    others(IMG)
    finish(TXT)

    for kind in (TXT, IMG):
        def done(j, carry, kind=kind):
            for copy in own_sends(kind, j):
                copy.wait_send()
            remote(from_slot, FWD, kind, j, fwd_sem.at[kind, j], other_core).wait_send()
            return carry

        lax.fori_loop(0, CHUNKS, done, 0)

    @pl.when(is_relay)
    def _():
        for kind in (TXT, IMG):
            for j in range(DIRECT, CHUNKS):
                relay_copy(kind, j).wait_send()

    for kind in (IMG, TXT):
        pltpu.make_async_copy(acc.at[kind], (image_out, text_out)[kind], out_sem.at[kind]).wait()


def local(image_embed, text_embed, logit_scale, logit_bias):
    rows, width = image_embed.shape
    whole = jax.ShapeDtypeStruct((rows, width), jnp.float32)
    n_red = 1 + (NY - 1) + (NX - 1) + (NZ - 1)
    return pl.pallas_call(
        kernel,
        name="window_loss",
        out_shape=(whole, whole, jax.ShapeDtypeStruct((1,), jnp.float32)),
        in_specs=[
            pl.BlockSpec(memory_space=pltpu.SMEM),
            pl.BlockSpec(memory_space=pltpu.SMEM),
            pl.BlockSpec(memory_space=pl.ANY),
            pl.BlockSpec(memory_space=pl.ANY),
        ],
        out_specs=(
            pl.BlockSpec(memory_space=pl.ANY),
            pl.BlockSpec(memory_space=pl.ANY),
            pl.BlockSpec(memory_space=pltpu.SMEM),
        ),
        scratch_shapes=[
            pltpu.VMEM((6, 2, rows, width), jnp.bfloat16),
            pltpu.VMEM((2, rows, width), jnp.float32),
            pltpu.VMEM((2, rows, 128), jnp.float32),
            pltpu.VMEM((2, rows, width), jnp.float32),
            pltpu.VMEM((8, 128), jnp.float32),
            pltpu.VMEM((2, 8, 128), jnp.float32),
            pltpu.VMEM((NY, 8, 128), jnp.float32),
            pltpu.VMEM((NZ, 8, 128), jnp.float32),
            pltpu.VMEM((NX, 8, 128), jnp.float32),
            pltpu.SemaphoreType.DMA((2,)),
            pltpu.SemaphoreType.DMA((2,)),
            pltpu.SemaphoreType.DMA((3, 2, CHUNKS)),
            pltpu.SemaphoreType.DMA((2, CHUNKS)),
            pltpu.SemaphoreType.DMA((2, CHUNKS)),
            pltpu.SemaphoreType.DMA((5, 2, CHUNKS)),
            pltpu.SemaphoreType.DMA((n_red,)),
            pltpu.SemaphoreType.DMA((n_red,)),
        ],
        compiler_params=pltpu.CompilerParams(
            collective_id=0, has_side_effects=True, vmem_limit_bytes=48 * 2**20
        ),
        cost_estimate=pl.CostEstimate(
            flops=20 * 2 * rows * rows * width,
            bytes_accessed=4 * 4 * rows * width,
            transcendentals=10 * rows * rows,
        ),
    )(logit_scale, logit_bias, image_embed, text_embed)


def solution(mesh):
    placed = (P(("blk", "group"), None), P(("blk", "group"), None), P(), P())
    return jax.shard_map(
        local,
        mesh=mesh,
        in_specs=placed,
        out_specs=(P(("blk", "group"), None), P(("blk", "group"), None), P()),
        check_vma=False,
    )
```

```python
import functools

import jax
import jax.numpy as jnp
from jax import lax
from jax.experimental import pallas as pl
from jax.experimental.pallas import tpu as pltpu
from jax.sharding import PartitionSpec as P

MESH = pl.DeviceIdType.MESH

NY, NX, ZH, ZL = 8, 4, 2, 6
NZ = ZH * ZL

UP, DN, SIB, FWD, RELAY, OWN = range(6)
IMG, TXT = 0, 1

CHUNKS = 4
DIRECT = 2
STRIP = 32


def kernel(
    scale_ref, bias_ref, image_hbm, text_hbm, image_out, text_out, scale_out,
    feat, raw, inv, acc, part, sum_c, sum_x, sum_y, sum_z, red_c, red_y, red_z, red_x, red_b,
    load_sem, out_sem, send_sem, fwd_sem, relay_sem, recv_sem, red_send, red_recv, turn_sem,
):
    rows, width = image_hbm.shape
    step = rows // CHUNKS
    b, g = lax.axis_index("blk"), lax.axis_index("group")
    zh, y, c = b // (2 * NY), (b // 2) % NY, b % 2
    x, zl = g // ZL, g % ZL
    z = zh * ZL + zl

    def dev(x, y, z, c):
        return ((z // ZL) * (2 * NY) + y * 2 + c, x * ZL + z % ZL)

    other_core = dev(x, y, z, 1 - c)
    far_z = (z + ZL) % NZ

    home = 2 + x
    at_home = y == home
    at_top, at_bottom = y == NY - 1, y == 0
    on_seam = at_top | at_bottom
    is_relay = (y == NY - 2) | (y == 1)
    barrier = pltpu.get_barrier_semaphore()

    def greet(device):
        pl.semaphore_signal(barrier, inc=1, device_id=device, device_id_type=MESH)

    @pl.when(on_seam)
    def _():
        greet(dev(x, NY - 1 - y, far_z, c))
        greet(dev(x, jnp.where(at_top, 1, NY - 2), far_z, c))

    @pl.when(is_relay)
    def _():
        greet(dev(x, jnp.where(y == 1, NY - 1, 0), far_z, c))

    @pl.when(on_seam | is_relay)
    def _():
        greet(dev(x, y, (z + 2) % NZ, c))
        greet(dev(x, y, (z + NZ - 2) % NZ, c))

    @pl.when(at_home)
    def _():
        for d in range(1, NZ):
            greet(dev(x, y, (z + d) % NZ, c))
        for d in range(1, NY):
            greet(dev(x, (y + d) % NY, z, c))

    @pl.when(jnp.logical_not(at_home))
    def _():
        greet(dev(x, home, z, c))

    @pl.when(jnp.logical_not(at_top))
    def _():
        greet(dev(x, (y + 1) % NY, z, c))

    @pl.when(jnp.logical_not(at_bottom))
    def _():
        greet(dev(x, (y + NY - 1) % NY, z, c))

    greet(other_core)
    for d in range(1, NX):
        greet(dev((x + d) % NX, y, z, c))
    n_greet = (
        NX
        + jnp.where(on_seam, 5, 2)
        + jnp.where(is_relay, 3, 0)
        + jnp.where(at_home, NZ + NY - 2, 1)
    )

    loads = [
        pltpu.make_async_copy(image_hbm, raw.at[IMG], load_sem.at[IMG]),
        pltpu.make_async_copy(text_hbm, raw.at[TXT], load_sem.at[TXT]),
    ]
    loads[TXT].start()
    loads[IMG].start()

    def normalize(kind):
        def strip(i, carry):
            at = pl.ds(pl.multiple_of(i * STRIP, STRIP), STRIP)
            value = raw[kind, at, :]
            scale = lax.rsqrt(jnp.sum(value * value, axis=1, keepdims=True) + 1e-06)
            inv[kind, at, :] = jnp.broadcast_to(scale, (STRIP, 128))
            feat[OWN, kind, at, :] = (value * scale).astype(jnp.bfloat16)
            return carry

        lax.fori_loop(0, rows // STRIP, strip, 0)

    def remote(src_slot, dst_slot, kind, j, send, device):
        at = pl.ds(pl.multiple_of(j * step, step), step)
        return pltpu.make_async_remote_copy(
            src_ref=feat.at[src_slot, kind, at],
            dst_ref=feat.at[dst_slot, kind, at],
            send_sem=send,
            recv_sem=recv_sem.at[dst_slot, kind, j],
            device_id=device,
            device_id_type=MESH,
        )

    def pick(cond, a, b):
        return jnp.where(cond, a, b)

    def seam_send(kind, j):
        hop = j >= DIRECT
        to_y = pick(hop, pick(at_top, NY - 2, 1), pick(at_top, 0, NY - 1))
        to_z = pick(hop, z, far_z)
        slot = pick(hop, RELAY, pick(at_top, DN, UP))
        return remote(OWN, slot, kind, j, send_sem.at[0, kind, j], dev(x, to_y, to_z, c))

    def up_send(kind, j):
        return remote(OWN, DN, kind, j, send_sem.at[0, kind, j], dev(x, (y + 1) % NY, z, c))

    def down_send(kind, j):
        return remote(OWN, UP, kind, j, send_sem.at[1, kind, j], dev(x, (y + NY - 1) % NY, z, c))

    def plain_send(kind, j):
        slot = pick(at_top, UP, DN)
        to_y = pick(at_top, NY - 2, 1)
        return remote(OWN, slot, kind, j, send_sem.at[1, kind, j], dev(x, to_y, z, c))

    def side_send(kind, j):
        return remote(OWN, SIB, kind, j, send_sem.at[2, kind, j], other_core)

    def each(n, action):
        def one(i, carry):
            action(i)
            return carry

        lax.fori_loop(0, n, one, 0)

    def send_legs(kind):
        @pl.when(on_seam)
        def _():
            for j in range(DIRECT, CHUNKS):
                seam_send(kind, j).start()

    def send_plain(kind):
        def one(j):
            @pl.when(on_seam)
            def _():
                plain_send(kind, j).start()

            @pl.when(jnp.logical_not(on_seam))
            def _():
                up_send(kind, j).start()
                down_send(kind, j).start()

            side_send(kind, j).start()

        each(CHUNKS, one)

    def relay_copy(kind, j):
        to_y = pick(y == NY - 2, 0, NY - 1)
        slot = pick(y == NY - 2, DN, UP)
        return remote(RELAY, slot, kind, j, relay_sem.at[kind, j], dev(x, to_y, far_z, c))

    def arrived(slot, kind, j):
        remote(OWN, slot, kind, j, fwd_sem.at[kind, j], other_core).wait_recv()

    from_slot = pick(c == 0, UP, DN)
    rest_slot = pick(c == 0, DN, UP)

    def pass_on(kind):
        def one(i, carry):
            j = i
            arrived(from_slot, kind, j)
            remote(from_slot, FWD, kind, j, fwd_sem.at[kind, j], other_core).start()
            return carry

        lax.fori_loop(0, CHUNKS, one, 0)

    def await_block(slot, kind):
        def one(j, carry):
            arrived(slot, kind, j)
            return carry

        lax.fori_loop(0, CHUNKS, one, 0)

    temper = scale_ref[0]
    offset = bias_ref[0]

    def pair(slot, kind, own):
        mine = 1 - kind
        inner = lax.dot_general(
            feat[OWN, mine], feat[slot, kind], (((1,), (1,)), ((), ())),
            preferred_element_type=jnp.float32,
        )
        logits = temper * inner + offset
        if own:
            r = lax.broadcasted_iota(jnp.int32, (rows, rows), 0)
            s = lax.broadcasted_iota(jnp.int32, (rows, rows), 1)
            sign = jnp.where(r == s, 1.0, -1.0)
            coeff = -sign / (1.0 + jnp.exp(sign * logits))
        else:
            coeff = 1.0 / (1.0 + jnp.exp(-logits))
        coeff = coeff.astype(jnp.bfloat16)
        term = jnp.dot(coeff, feat[slot, kind], preferred_element_type=jnp.float32)
        if own:
            acc[mine] = term
        else:
            acc[mine] += term
        if kind == TXT:
            share = coeff.astype(jnp.float32) * inner
            share = jnp.sum(share.reshape(rows // 8, 8, rows), axis=0)
            share = share[:, :128] + share[:, 128:]
            if own:
                part[...] = share
            else:
                part[...] += share

    def finish(kind):
        out = (image_out, text_out)[kind]

        def strip(i, carry):
            at = pl.ds(pl.multiple_of(i * STRIP, STRIP), STRIP)
            scale = inv[kind, at, :][:, :1]
            unit = raw[kind, at, :] * scale
            direction = temper * acc[kind, at, :]
            along = jnp.sum(unit * direction, axis=1, keepdims=True)
            acc[kind, at, :] = scale * (direction - unit * along)
            return carry

        lax.fori_loop(0, rows // STRIP, strip, 0)
        pltpu.make_async_copy(acc.at[kind], out, out_sem.at[kind]).start()

    def total_of(buf, n):
        total = buf[0]
        for i in range(1, n):
            total = total + buf[i]
        return total

    def share_copy(src, buf, at, k, device):
        return pltpu.make_async_remote_copy(
            src_ref=src, dst_ref=buf.at[at], send_sem=red_send.at[k], recv_sem=red_recv.at[k],
            device_id=device, device_id_type=MESH,
        )

    def reduce_over(src, dst, buf, n, me, at, base):
        buf[me] = src[...]
        copies = [share_copy(src, buf, me, base + d, at((me + d) % n)) for d in range(1, n)]
        for copy in copies:
            copy.start()
        for copy in copies:
            copy.wait()
        dst[...] = total_of(buf, n)

    K_C, K_X, K_Y, K_Z, K_B = 0, 2, 2 + NX, 2 + NX + NY, 2 + NX + NY + NZ

    def gather_copy():
        return share_copy(sum_x, red_y, y, K_Y + y, dev(x, home, z, c))

    def spread_copy(to):
        return share_copy(sum_z, red_b, 0, K_B + to, dev(x, to, z, c))

    def home_sums():
        red_y[y] = sum_x[...]
        for d in range(1, NY):
            k = (y + d) % NY
            share_copy(sum_x, red_y, k, K_Y + k, other_core).wait_recv()
        sum_y[...] = total_of(red_y, NY)
        reduce_over(sum_y, sum_z, red_z, NZ, z, lambda i: dev(x, y, i, c), K_Z)
        for d in range(1, NY):
            spread_copy((y + d) % NY).start()

    with jax.named_scope("text_load"):
        loads[TXT].wait()
        normalize(TXT)
    with jax.named_scope("greeting"):
        pl.semaphore_wait(barrier, n_greet)
    with jax.named_scope("sends"):
        send_legs(TXT)
        loads[IMG].wait()
        normalize(IMG)
        send_legs(IMG)
        send_plain(TXT)

    phase = (z // 2) % 3
    after = dev(x, y, (z + 2) % NZ, c)

    def take_turn(kind):
        def await_turn():
            pl.semaphore_wait(turn_sem, 1)

        def pass_turn():
            pl.semaphore_signal(turn_sem, inc=1, device_id=after, device_id_type=MESH)

        @pl.when(on_seam | is_relay)
        def _():
            if kind == TXT:
                pl.when(phase > 0)(await_turn)
            else:
                await_turn()

        @pl.when(on_seam)
        def _():
            for j in range(DIRECT):
                seam_send(kind, j).start()
            seam_send(kind, 0).wait_send()

        @pl.when(is_relay)
        def _():
            for j in range(DIRECT, CHUNKS):
                arrived(RELAY, kind, j)
                relay_copy(kind, j).start()
            relay_copy(kind, DIRECT).wait_send()

        @pl.when(on_seam | is_relay)
        def _():
            if kind == TXT:
                pass_turn()
            else:
                pl.when(phase < 2)(pass_turn)

    pl.when(phase == 0)(lambda: take_turn(TXT))
    with jax.named_scope("own_pair"):
        pair(OWN, TXT, True)
    pl.when(phase > 0)(lambda: take_turn(TXT))
    pair(OWN, IMG, True)

    def others(kind):
        with jax.named_scope("sibling"):
            await_block(SIB, kind)
            pair(SIB, kind, False)
        with jax.named_scope("pass_on"):
            pass_on(kind)
        with jax.named_scope("passed_pair"):
            pair(from_slot, kind, False)

        def one(i, carry):
            slot = pick(i == 0, rest_slot, FWD)
            with jax.named_scope("wait"):
                await_block(slot, kind)
            pair(slot, kind, False)
            return carry

        with jax.named_scope("rest"):
            lax.fori_loop(0, 2, one, 0)

    others(TXT)
    reduce_over(part, sum_c, red_c, 2, c, lambda i: dev(x, y, z, i), K_C)
    reduce_over(sum_c, sum_x, red_x, NX, x, lambda i: dev(i, y, z, c), K_X)

    @pl.when(jnp.logical_not(at_home))
    def _():
        gather_copy().start()

    send_plain(IMG)
    take_turn(IMG)

    @pl.when(at_home)
    def _():
        home_sums()

    finish(IMG)
    others(IMG)
    with jax.named_scope("finish_text"):
        finish(TXT)

    scaled = 1.0 / (rows * NX * NY * NZ * 2)

    @pl.when(at_home)
    def _():
        scale_out[0] = jnp.sum(sum_z[...]) * scaled
        for d in range(1, NY):
            spread_copy((y + d) % NY).wait_send()

    @pl.when(jnp.logical_not(at_home))
    def _():
        spread_copy(y).wait_recv()
        scale_out[0] = jnp.sum(red_b[0]) * scaled
        gather_copy().wait_send()

    with jax.named_scope("sent"):
        def sent(n, kind, j):
            remote(OWN, SIB, kind, j, send_sem.at[n, kind, j], other_core).wait_send()

        for kind in (TXT, IMG):
            for j in range(CHUNKS):
                sent(1, kind, j)
                sent(2, kind, j)
                remote(from_slot, FWD, kind, j, fwd_sem.at[kind, j], other_core).wait_send()
                if j == 0:
                    pl.when(jnp.logical_not(on_seam))(lambda: sent(0, kind, 0))
                else:
                    sent(0, kind, j)

        @pl.when(is_relay)
        def _():
            for kind in (TXT, IMG):
                for j in range(DIRECT + 1, CHUNKS):
                    relay_copy(kind, j).wait_send()

    for kind in (IMG, TXT):
        pltpu.make_async_copy(acc.at[kind], (image_out, text_out)[kind], out_sem.at[kind]).wait()


def local(image_embed, text_embed, logit_scale, logit_bias):
    rows, width = image_embed.shape
    whole = jax.ShapeDtypeStruct((rows, width), jnp.float32)
    n_red = 2 + NX + 2 * NY + NZ
    return pl.pallas_call(
        kernel,
        name="window_loss",
        out_shape=(whole, whole, jax.ShapeDtypeStruct((1,), jnp.float32)),
        in_specs=[
            pl.BlockSpec(memory_space=pltpu.SMEM),
            pl.BlockSpec(memory_space=pltpu.SMEM),
            pl.BlockSpec(memory_space=pl.ANY),
            pl.BlockSpec(memory_space=pl.ANY),
        ],
        out_specs=(
            pl.BlockSpec(memory_space=pl.ANY),
            pl.BlockSpec(memory_space=pl.ANY),
            pl.BlockSpec(memory_space=pltpu.SMEM),
        ),
        scratch_shapes=[
            pltpu.VMEM((6, 2, rows, width), jnp.bfloat16),
            pltpu.VMEM((2, rows, width), jnp.float32),
            pltpu.VMEM((2, rows, 128), jnp.float32),
            pltpu.VMEM((2, rows, width), jnp.float32),
            *[pltpu.VMEM((8, 128), jnp.float32)] * 5,
            pltpu.VMEM((2, 8, 128), jnp.float32),
            pltpu.VMEM((NY, 8, 128), jnp.float32),
            pltpu.VMEM((NZ, 8, 128), jnp.float32),
            pltpu.VMEM((NX, 8, 128), jnp.float32),
            pltpu.VMEM((1, 8, 128), jnp.float32),
            pltpu.SemaphoreType.DMA((2,)),
            pltpu.SemaphoreType.DMA((2,)),
            pltpu.SemaphoreType.DMA((3, 2, CHUNKS)),
            pltpu.SemaphoreType.DMA((2, CHUNKS)),
            pltpu.SemaphoreType.DMA((2, CHUNKS)),
            pltpu.SemaphoreType.DMA((5, 2, CHUNKS)),
            pltpu.SemaphoreType.DMA((n_red,)),
            pltpu.SemaphoreType.DMA((n_red,)),
            pltpu.SemaphoreType.REGULAR,
        ],
        compiler_params=pltpu.CompilerParams(
            collective_id=0, has_side_effects=True, vmem_limit_bytes=60 * 2**20
        ),
        cost_estimate=pl.CostEstimate(
            flops=20 * 2 * rows * rows * width,
            bytes_accessed=4 * 4 * rows * width,
            transcendentals=10 * rows * rows,
        ),
    )(logit_scale, logit_bias, image_embed, text_embed)


def solution(mesh):
    placed = (P(("blk", "group"), None), P(("blk", "group"), None), P(), P())
    return jax.shard_map(
        local,
        mesh=mesh,
        in_specs=placed,
        out_specs=(P(("blk", "group"), None), P(("blk", "group"), None), P()),
        check_vma=False,
    )
```

```python
import functools

import jax
import jax.numpy as jnp
from jax import lax
from jax.experimental import pallas as pl
from jax.experimental.pallas import tpu as pltpu
from jax.sharding import PartitionSpec as P

MESH = pl.DeviceIdType.MESH

NY, NX, ZH, ZL = 8, 4, 2, 6
NZ = ZH * ZL

UP, DN, SIB, FWD, RELAY, OWN = range(6)
IMG, TXT = 0, 1

CHUNKS = 4
DIRECT = 2
STRIP = 32


def kernel(
    scale_ref, bias_ref, image_hbm, text_hbm, image_out, text_out, scale_out,
    feat, raw, inv, acc, part, sum_c, sum_x, sum_y, sum_z, red_c, red_y, red_z, red_x, red_b,
    load_sem, out_sem, send_sem, fwd_sem, relay_sem, recv_sem, red_send, red_recv, turn_sem,
):
    rows, width = image_hbm.shape
    step = rows // CHUNKS
    b, g = lax.axis_index("blk"), lax.axis_index("group")
    zh, y, c = b // (2 * NY), (b // 2) % NY, b % 2
    x, zl = g // ZL, g % ZL
    z = zh * ZL + zl

    def dev(x, y, z, c):
        return ((z // ZL) * (2 * NY) + y * 2 + c, x * ZL + z % ZL)

    other_core = dev(x, y, z, 1 - c)
    far_z = (z + ZL) % NZ

    home = 3 + x % 2
    at_home = y == home
    at_top, at_bottom = y == NY - 1, y == 0
    on_seam = at_top | at_bottom
    is_relay = (y == NY - 2) | (y == 1)
    barrier = pltpu.get_barrier_semaphore()

    def greet(device):
        pl.semaphore_signal(barrier, inc=1, device_id=device, device_id_type=MESH)

    @pl.when(on_seam)
    def _():
        greet(dev(x, NY - 1 - y, far_z, c))
        greet(dev(x, jnp.where(at_top, 1, NY - 2), far_z, c))

    @pl.when(is_relay)
    def _():
        greet(dev(x, jnp.where(y == 1, NY - 1, 0), far_z, c))

    @pl.when(on_seam | is_relay)
    def _():
        greet(dev(x, y, (z + 2) % NZ, c))
        greet(dev(x, y, (z + NZ - 2) % NZ, c))

    @pl.when(at_home)
    def _():
        for d in range(1, NZ):
            greet(dev(x, y, (z + d) % NZ, c))
        for d in range(1, NY):
            greet(dev(x, (y + d) % NY, z, c))

    @pl.when(jnp.logical_not(at_home))
    def _():
        greet(dev(x, home, z, c))

    @pl.when(jnp.logical_not(at_top))
    def _():
        greet(dev(x, (y + 1) % NY, z, c))

    @pl.when(jnp.logical_not(at_bottom))
    def _():
        greet(dev(x, (y + NY - 1) % NY, z, c))

    greet(other_core)
    for d in range(1, NX):
        greet(dev((x + d) % NX, y, z, c))
    n_greet = (
        NX
        + jnp.where(on_seam, 5, 2)
        + jnp.where(is_relay, 3, 0)
        + jnp.where(at_home, NZ + NY - 2, 1)
    )

    loads = [
        pltpu.make_async_copy(image_hbm, raw.at[IMG], load_sem.at[IMG]),
        pltpu.make_async_copy(text_hbm, raw.at[TXT], load_sem.at[TXT]),
    ]
    loads[TXT].start()
    loads[IMG].start()

    def normalize(kind):
        def strip(i, carry):
            at = pl.ds(pl.multiple_of(i * STRIP, STRIP), STRIP)
            value = raw[kind, at, :]
            scale = lax.rsqrt(jnp.sum(value * value, axis=1, keepdims=True) + 1e-06)
            inv[kind, at, :] = jnp.broadcast_to(scale, (STRIP, 128))
            feat[OWN, kind, at, :] = (value * scale).astype(jnp.bfloat16)
            return carry

        lax.fori_loop(0, rows // STRIP, strip, 0)

    def remote(src_slot, dst_slot, kind, j, send, device):
        at = pl.ds(pl.multiple_of(j * step, step), step)
        return pltpu.make_async_remote_copy(
            src_ref=feat.at[src_slot, kind, at],
            dst_ref=feat.at[dst_slot, kind, at],
            send_sem=send,
            recv_sem=recv_sem.at[dst_slot, kind, j],
            device_id=device,
            device_id_type=MESH,
        )

    def pick(cond, a, b):
        return jnp.where(cond, a, b)

    def seam_send(kind, j):
        hop = j >= DIRECT
        to_y = pick(hop, pick(at_top, NY - 2, 1), pick(at_top, 0, NY - 1))
        to_z = pick(hop, z, far_z)
        slot = pick(hop, RELAY, pick(at_top, DN, UP))
        return remote(OWN, slot, kind, j, send_sem.at[0, kind, j], dev(x, to_y, to_z, c))

    def up_send(kind, j):
        return remote(OWN, DN, kind, j, send_sem.at[0, kind, j], dev(x, (y + 1) % NY, z, c))

    def down_send(kind, j):
        return remote(OWN, UP, kind, j, send_sem.at[1, kind, j], dev(x, (y + NY - 1) % NY, z, c))

    def plain_send(kind, j):
        slot = pick(at_top, UP, DN)
        to_y = pick(at_top, NY - 2, 1)
        return remote(OWN, slot, kind, j, send_sem.at[1, kind, j], dev(x, to_y, z, c))

    def side_send(kind, j):
        return remote(OWN, SIB, kind, j, send_sem.at[2, kind, j], other_core)

    def each(n, action):
        def one(i, carry):
            action(i)
            return carry

        lax.fori_loop(0, n, one, 0)

    def send_legs(kind):
        @pl.when(on_seam)
        def _():
            for j in range(DIRECT, CHUNKS):
                seam_send(kind, j).start()

    def send_plain(kind):
        def one(j):
            @pl.when(on_seam)
            def _():
                plain_send(kind, j).start()

            @pl.when(jnp.logical_not(on_seam))
            def _():
                up_send(kind, j).start()
                down_send(kind, j).start()

            side_send(kind, j).start()

        each(CHUNKS, one)

    def relay_copy(kind, j):
        to_y = pick(y == NY - 2, 0, NY - 1)
        slot = pick(y == NY - 2, DN, UP)
        return remote(RELAY, slot, kind, j, relay_sem.at[kind, j], dev(x, to_y, far_z, c))

    def arrived(slot, kind, j):
        remote(OWN, slot, kind, j, fwd_sem.at[kind, j], other_core).wait_recv()

    from_slot = pick(c == 0, UP, DN)
    rest_slot = pick(c == 0, DN, UP)

    def pass_on(kind):
        def one(i, carry):
            j = i
            arrived(from_slot, kind, j)
            remote(from_slot, FWD, kind, j, fwd_sem.at[kind, j], other_core).start()
            return carry

        lax.fori_loop(0, CHUNKS, one, 0)

    def await_block(slot, kind):
        def one(j, carry):
            arrived(slot, kind, j)
            return carry

        lax.fori_loop(0, CHUNKS, one, 0)

    temper = scale_ref[0]
    offset = bias_ref[0]

    def pair(slot, kind, own):
        mine = 1 - kind
        inner = lax.dot_general(
            feat[OWN, mine], feat[slot, kind], (((1,), (1,)), ((), ())),
            preferred_element_type=jnp.float32,
        )
        logits = temper * inner + offset
        if own:
            r = lax.broadcasted_iota(jnp.int32, (rows, rows), 0)
            s = lax.broadcasted_iota(jnp.int32, (rows, rows), 1)
            sign = jnp.where(r == s, 1.0, -1.0)
            coeff = -sign / (1.0 + jnp.exp(sign * logits))
        else:
            coeff = 1.0 / (1.0 + jnp.exp(-logits))
        coeff = coeff.astype(jnp.bfloat16)
        term = jnp.dot(coeff, feat[slot, kind], preferred_element_type=jnp.float32)
        if own:
            acc[mine] = term
        else:
            acc[mine] += term
        if kind == TXT:
            share = coeff.astype(jnp.float32) * inner
            share = jnp.sum(share.reshape(rows // 8, 8, rows), axis=0)
            share = share[:, :128] + share[:, 128:]
            if own:
                part[...] = share
            else:
                part[...] += share

    def finish(kind):
        out = (image_out, text_out)[kind]

        def strip(i, carry):
            at = pl.ds(pl.multiple_of(i * STRIP, STRIP), STRIP)
            scale = inv[kind, at, :][:, :1]
            unit = raw[kind, at, :] * scale
            direction = temper * acc[kind, at, :]
            along = jnp.sum(unit * direction, axis=1, keepdims=True)
            acc[kind, at, :] = scale * (direction - unit * along)
            return carry

        lax.fori_loop(0, rows // STRIP, strip, 0)
        pltpu.make_async_copy(acc.at[kind], out, out_sem.at[kind]).start()

    def total_of(buf, n):
        total = buf[0]
        for i in range(1, n):
            total = total + buf[i]
        return total

    def share_copy(src, buf, at, k, device):
        return pltpu.make_async_remote_copy(
            src_ref=src, dst_ref=buf.at[at], send_sem=red_send.at[k], recv_sem=red_recv.at[k],
            device_id=device, device_id_type=MESH,
        )

    def reduce_over(src, dst, buf, n, me, at, base):
        buf[me] = src[...]
        copies = [share_copy(src, buf, me, base + d, at((me + d) % n)) for d in range(1, n)]
        for copy in copies:
            copy.start()
        for copy in copies:
            copy.wait()
        dst[...] = total_of(buf, n)

    K_C, K_X, K_Y, K_Z, K_B = 0, 2, 2 + NX, 2 + NX + NY, 2 + NX + NY + NZ

    def gather_copy():
        return share_copy(sum_x, red_y, y, K_Y + y, dev(x, home, z, c))

    def spread_copy(to):
        return share_copy(sum_z, red_b, 0, K_B + to, dev(x, to, z, c))

    def home_sums():
        red_y[y] = sum_x[...]
        for d in range(1, NY):
            k = (y + d) % NY
            share_copy(sum_x, red_y, k, K_Y + k, other_core).wait_recv()
        sum_y[...] = total_of(red_y, NY)
        reduce_over(sum_y, sum_z, red_z, NZ, z, lambda i: dev(x, y, i, c), K_Z)
        for d in range(1, NY):
            spread_copy((y + d) % NY).start()

    with jax.named_scope("text_load"):
        loads[TXT].wait()
        normalize(TXT)
    with jax.named_scope("greeting"):
        pl.semaphore_wait(barrier, n_greet)
    with jax.named_scope("sends"):
        send_legs(TXT)
        loads[IMG].wait()
        normalize(IMG)
        send_plain(TXT)
        send_legs(IMG)

    phase = (z // 2) % 3
    after = dev(x, y, (z + 2) % NZ, c)

    def take_turn(kind):
        def await_turn():
            pl.semaphore_wait(turn_sem, 1)

        def pass_turn():
            pl.semaphore_signal(turn_sem, inc=1, device_id=after, device_id_type=MESH)

        @pl.when(on_seam | is_relay)
        def _():
            if kind == TXT:
                pl.when(phase > 0)(await_turn)
            else:
                await_turn()

        @pl.when(on_seam)
        def _():
            for j in range(DIRECT):
                seam_send(kind, j).start()
            seam_send(kind, 0).wait_send()

        @pl.when(is_relay)
        def _():
            for j in range(DIRECT, CHUNKS):
                arrived(RELAY, kind, j)
                relay_copy(kind, j).start()
            relay_copy(kind, DIRECT).wait_send()

        @pl.when(on_seam | is_relay)
        def _():
            if kind == TXT:
                pass_turn()
            else:
                pl.when(phase < 2)(pass_turn)

    pl.when(phase == 0)(lambda: take_turn(TXT))
    with jax.named_scope("own_pair"):
        pair(OWN, TXT, True)
    pl.when(phase > 0)(lambda: take_turn(TXT))
    pair(OWN, IMG, True)

    crossing = (at_top & (c == 0)) | (at_bottom & (c == 1))

    def others(kind):
        def rest():
            await_block(rest_slot, kind)
            pair(rest_slot, kind, False)

        await_block(SIB, kind)
        pair(SIB, kind, False)
        if kind == IMG:
            pl.when(crossing)(rest)
        pass_on(kind)
        pair(from_slot, kind, False)
        if kind == IMG:
            pl.when(jnp.logical_not(crossing))(rest)
        else:
            rest()
        await_block(FWD, kind)
        pair(FWD, kind, False)

    others(TXT)
    early = is_relay & (phase < 1)
    pl.when(early)(lambda: take_turn(IMG))
    reduce_over(part, sum_c, red_c, 2, c, lambda i: dev(x, y, z, i), K_C)
    reduce_over(sum_c, sum_x, red_x, NX, x, lambda i: dev(i, y, z, c), K_X)

    @pl.when(jnp.logical_not(at_home))
    def _():
        gather_copy().start()

    send_plain(IMG)
    pl.when(jnp.logical_not(early))(lambda: take_turn(IMG))

    finish(IMG)
    others(IMG)

    @pl.when(at_home)
    def _():
        home_sums()

    with jax.named_scope("finish_text"):
        finish(TXT)

    scaled = 1.0 / (rows * NX * NY * NZ * 2)

    @pl.when(at_home)
    def _():
        scale_out[0] = jnp.sum(sum_z[...]) * scaled
        for d in range(1, NY):
            spread_copy((y + d) % NY).wait_send()

    @pl.when(jnp.logical_not(at_home))
    def _():
        spread_copy(y).wait_recv()
        scale_out[0] = jnp.sum(red_b[0]) * scaled
        gather_copy().wait_send()

    with jax.named_scope("sent"):
        def sent(n, kind, j):
            remote(OWN, SIB, kind, j, send_sem.at[n, kind, j], other_core).wait_send()

        for kind in (TXT, IMG):
            for j in range(CHUNKS):
                sent(1, kind, j)
                sent(2, kind, j)
                remote(from_slot, FWD, kind, j, fwd_sem.at[kind, j], other_core).wait_send()
                if j == 0:
                    pl.when(jnp.logical_not(on_seam))(lambda: sent(0, kind, 0))
                else:
                    sent(0, kind, j)

        @pl.when(is_relay)
        def _():
            for kind in (TXT, IMG):
                for j in range(DIRECT + 1, CHUNKS):
                    relay_copy(kind, j).wait_send()

    for kind in (IMG, TXT):
        pltpu.make_async_copy(acc.at[kind], (image_out, text_out)[kind], out_sem.at[kind]).wait()


def local(image_embed, text_embed, logit_scale, logit_bias):
    rows, width = image_embed.shape
    whole = jax.ShapeDtypeStruct((rows, width), jnp.float32)
    n_red = 2 + NX + 2 * NY + NZ
    return pl.pallas_call(
        kernel,
        name="window_loss",
        out_shape=(whole, whole, jax.ShapeDtypeStruct((1,), jnp.float32)),
        in_specs=[
            pl.BlockSpec(memory_space=pltpu.SMEM),
            pl.BlockSpec(memory_space=pltpu.SMEM),
            pl.BlockSpec(memory_space=pl.ANY),
            pl.BlockSpec(memory_space=pl.ANY),
        ],
        out_specs=(
            pl.BlockSpec(memory_space=pl.ANY),
            pl.BlockSpec(memory_space=pl.ANY),
            pl.BlockSpec(memory_space=pltpu.SMEM),
        ),
        scratch_shapes=[
            pltpu.VMEM((6, 2, rows, width), jnp.bfloat16),
            pltpu.VMEM((2, rows, width), jnp.float32),
            pltpu.VMEM((2, rows, 128), jnp.float32),
            pltpu.VMEM((2, rows, width), jnp.float32),
            *[pltpu.VMEM((8, 128), jnp.float32)] * 5,
            pltpu.VMEM((2, 8, 128), jnp.float32),
            pltpu.VMEM((NY, 8, 128), jnp.float32),
            pltpu.VMEM((NZ, 8, 128), jnp.float32),
            pltpu.VMEM((NX, 8, 128), jnp.float32),
            pltpu.VMEM((1, 8, 128), jnp.float32),
            pltpu.SemaphoreType.DMA((2,)),
            pltpu.SemaphoreType.DMA((2,)),
            pltpu.SemaphoreType.DMA((3, 2, CHUNKS)),
            pltpu.SemaphoreType.DMA((2, CHUNKS)),
            pltpu.SemaphoreType.DMA((2, CHUNKS)),
            pltpu.SemaphoreType.DMA((5, 2, CHUNKS)),
            pltpu.SemaphoreType.DMA((n_red,)),
            pltpu.SemaphoreType.DMA((n_red,)),
            pltpu.SemaphoreType.REGULAR,
        ],
        compiler_params=pltpu.CompilerParams(
            collective_id=0, has_side_effects=True, vmem_limit_bytes=60 * 2**20
        ),
        cost_estimate=pl.CostEstimate(
            flops=20 * 2 * rows * rows * width,
            bytes_accessed=4 * 4 * rows * width,
            transcendentals=10 * rows * rows,
        ),
    )(logit_scale, logit_bias, image_embed, text_embed)


def solution(mesh):
    placed = (P(("blk", "group"), None), P(("blk", "group"), None), P(), P())
    return jax.shard_map(
        local,
        mesh=mesh,
        in_specs=placed,
        out_specs=(P(("blk", "group"), None), P(("blk", "group"), None), P()),
        check_vma=False,
    )
```

```python
import functools

import jax
import jax.numpy as jnp
from jax import lax
from jax.experimental import pallas as pl
from jax.experimental.pallas import tpu as pltpu
from jax.sharding import PartitionSpec as P

MESH = pl.DeviceIdType.MESH

NY, NX, ZH, ZL = 8, 4, 2, 6
NZ = ZH * ZL

UP, DN, SIB, FWD, RELAY, OWN = range(6)
IMG, TXT = 0, 1

CHUNKS = 4
DIRECT = 2
STRIP = 32


def kernel(
    scale_ref, bias_ref, image_hbm, text_hbm, image_out, text_out, scale_out,
    feat, raw, inv, acc, part, sum_c, sum_x, sum_y, sum_z, red_c, red_y, red_z, red_x, red_b,
    load_sem, out_sem, send_sem, fwd_sem, relay_sem, recv_sem, red_send, red_recv, turn_sem,
):
    rows, width = image_hbm.shape
    step = rows // CHUNKS
    b, g = lax.axis_index("blk"), lax.axis_index("group")
    zh, y, c = b // (2 * NY), (b // 2) % NY, b % 2
    x, zl = g // ZL, g % ZL
    z = zh * ZL + zl

    def dev(x, y, z, c):
        return ((z // ZL) * (2 * NY) + y * 2 + c, x * ZL + z % ZL)

    other_core = dev(x, y, z, 1 - c)
    far_z = (z + ZL) % NZ

    home = 3 + x % 2
    at_home = y == home
    at_top, at_bottom = y == NY - 1, y == 0
    on_seam = at_top | at_bottom
    is_relay = (y == NY - 2) | (y == 1)
    barrier = pltpu.get_barrier_semaphore()

    def greet(device):
        pl.semaphore_signal(barrier, inc=1, device_id=device, device_id_type=MESH)

    @pl.when(on_seam)
    def _():
        greet(dev(x, NY - 1 - y, far_z, c))
        greet(dev(x, jnp.where(at_top, 1, NY - 2), far_z, c))

    @pl.when(is_relay)
    def _():
        greet(dev(x, jnp.where(y == 1, NY - 1, 0), far_z, c))

    @pl.when(on_seam | is_relay)
    def _():
        greet(dev(x, y, (z + 2) % NZ, c))
        greet(dev(x, y, (z + NZ - 2) % NZ, c))

    @pl.when(at_home)
    def _():
        for d in range(1, NZ):
            greet(dev(x, y, (z + d) % NZ, c))
        for d in range(1, NY):
            greet(dev(x, (y + d) % NY, z, c))

    @pl.when(jnp.logical_not(at_home))
    def _():
        greet(dev(x, home, z, c))

    @pl.when(jnp.logical_not(at_top))
    def _():
        greet(dev(x, (y + 1) % NY, z, c))

    @pl.when(jnp.logical_not(at_bottom))
    def _():
        greet(dev(x, (y + NY - 1) % NY, z, c))

    greet(other_core)
    for d in range(1, NX):
        greet(dev((x + d) % NX, y, z, c))
    n_greet = (
        NX
        + jnp.where(on_seam, 5, 2)
        + jnp.where(is_relay, 3, 0)
        + jnp.where(at_home, NZ + NY - 2, 1)
    )

    loads = [
        pltpu.make_async_copy(image_hbm, raw.at[IMG], load_sem.at[IMG]),
        pltpu.make_async_copy(text_hbm, raw.at[TXT], load_sem.at[TXT]),
    ]
    loads[TXT].start()
    loads[IMG].start()

    def normalize(kind):
        def strip(i, carry):
            at = pl.ds(pl.multiple_of(i * STRIP, STRIP), STRIP)
            value = raw[kind, at, :]
            scale = lax.rsqrt(jnp.sum(value * value, axis=1, keepdims=True) + 1e-06)
            inv[kind, at, :] = jnp.broadcast_to(scale, (STRIP, 128))
            feat[OWN, kind, at, :] = (value * scale).astype(jnp.bfloat16)
            return carry

        lax.fori_loop(0, rows // STRIP, strip, 0)

    def remote(src_slot, dst_slot, kind, j, send, device):
        at = pl.ds(pl.multiple_of(j * step, step), step)
        return pltpu.make_async_remote_copy(
            src_ref=feat.at[src_slot, kind, at],
            dst_ref=feat.at[dst_slot, kind, at],
            send_sem=send,
            recv_sem=recv_sem.at[dst_slot, kind, j],
            device_id=device,
            device_id_type=MESH,
        )

    def pick(cond, a, b):
        return jnp.where(cond, a, b)

    def seam_send(kind, j):
        hop = j >= DIRECT
        to_y = pick(hop, pick(at_top, NY - 2, 1), pick(at_top, 0, NY - 1))
        to_z = pick(hop, z, far_z)
        slot = pick(hop, RELAY, pick(at_top, DN, UP))
        return remote(OWN, slot, kind, j, send_sem.at[0, kind, j], dev(x, to_y, to_z, c))

    def up_send(kind, j):
        return remote(OWN, DN, kind, j, send_sem.at[0, kind, j], dev(x, (y + 1) % NY, z, c))

    def down_send(kind, j):
        return remote(OWN, UP, kind, j, send_sem.at[1, kind, j], dev(x, (y + NY - 1) % NY, z, c))

    def plain_send(kind, j):
        slot = pick(at_top, UP, DN)
        to_y = pick(at_top, NY - 2, 1)
        return remote(OWN, slot, kind, j, send_sem.at[1, kind, j], dev(x, to_y, z, c))

    def side_send(kind, j):
        return remote(OWN, SIB, kind, j, send_sem.at[2, kind, j], other_core)

    def each(n, action):
        def one(i, carry):
            action(i)
            return carry

        lax.fori_loop(0, n, one, 0)

    def send_legs(kind):
        @pl.when(on_seam)
        def _():
            for j in range(DIRECT, CHUNKS):
                seam_send(kind, j).start()

    def send_plain(kind):
        def one(j):
            @pl.when(on_seam)
            def _():
                plain_send(kind, j).start()

            @pl.when(jnp.logical_not(on_seam))
            def _():
                up_send(kind, j).start()
                down_send(kind, j).start()

            side_send(kind, j).start()

        each(CHUNKS, one)

    def relay_copy(kind, j):
        to_y = pick(y == NY - 2, 0, NY - 1)
        slot = pick(y == NY - 2, DN, UP)
        return remote(RELAY, slot, kind, j, relay_sem.at[kind, j], dev(x, to_y, far_z, c))

    def arrived(slot, kind, j):
        remote(OWN, slot, kind, j, fwd_sem.at[kind, j], other_core).wait_recv()

    from_slot = pick(c == 0, UP, DN)
    rest_slot = pick(c == 0, DN, UP)

    def pass_on(kind):
        def one(i, carry):
            j = i
            arrived(from_slot, kind, j)
            remote(from_slot, FWD, kind, j, fwd_sem.at[kind, j], other_core).start()
            return carry

        lax.fori_loop(0, CHUNKS, one, 0)

    def await_block(slot, kind):
        def one(j, carry):
            arrived(slot, kind, j)
            return carry

        lax.fori_loop(0, CHUNKS, one, 0)

    temper = scale_ref[0]
    offset = bias_ref[0]

    def pair(slot, kind, own):
        mine = 1 - kind
        inner = lax.dot_general(
            feat[OWN, mine], feat[slot, kind], (((1,), (1,)), ((), ())),
            preferred_element_type=jnp.float32,
        )
        logits = temper * inner + offset
        if own:
            r = lax.broadcasted_iota(jnp.int32, (rows, rows), 0)
            s = lax.broadcasted_iota(jnp.int32, (rows, rows), 1)
            sign = jnp.where(r == s, 1.0, -1.0)
            coeff = -sign / (1.0 + jnp.exp(sign * logits))
        else:
            coeff = 1.0 / (1.0 + jnp.exp(-logits))
        coeff = coeff.astype(jnp.bfloat16)
        term = jnp.dot(coeff, feat[slot, kind], preferred_element_type=jnp.float32)
        if own:
            acc[mine] = term
        else:
            acc[mine] += term
        if kind == TXT:
            share = coeff.astype(jnp.float32) * inner
            share = jnp.sum(share.reshape(rows // 8, 8, rows), axis=0)
            share = share[:, :128] + share[:, 128:]
            if own:
                part[...] = share
            else:
                part[...] += share

    half = rows // 2

    def finish(kind):
        out = (image_out, text_out)[kind]

        def strip(i, carry):
            at = pl.ds(pl.multiple_of(i * STRIP, STRIP), STRIP)
            scale = inv[kind, at, :][:, :1]
            unit = raw[kind, at, :] * scale
            direction = temper * acc[kind, at, :]
            along = jnp.sum(unit * direction, axis=1, keepdims=True)
            acc[kind, at, :] = scale * (direction - unit * along)
            return carry

        for h in range(2):
            lax.fori_loop(h * half // STRIP, (h + 1) * half // STRIP, strip, 0)
            at = pl.ds(h * half, half)
            pltpu.make_async_copy(acc.at[kind, at], out.at[at], out_sem.at[kind, h]).start()

    def total_of(buf, n):
        total = buf[0]
        for i in range(1, n):
            total = total + buf[i]
        return total

    def share_copy(src, buf, at, k, device):
        return pltpu.make_async_remote_copy(
            src_ref=src, dst_ref=buf.at[at], send_sem=red_send.at[k], recv_sem=red_recv.at[k],
            device_id=device, device_id_type=MESH,
        )

    def reduce_over(src, dst, buf, n, me, at, base):
        buf[me] = src[...]
        copies = [share_copy(src, buf, me, base + d, at((me + d) % n)) for d in range(1, n)]
        for copy in copies:
            copy.start()
        for copy in copies:
            copy.wait()
        dst[...] = total_of(buf, n)

    K_C, K_X, K_Y, K_Z, K_B = 0, 2, 2 + NX, 2 + NX + NY, 2 + NX + NY + NZ

    def gather_copy():
        return share_copy(sum_x, red_y, y, K_Y + y, dev(x, home, z, c))

    def spread_copy(to):
        return share_copy(sum_z, red_b, 0, K_B + to, dev(x, to, z, c))

    def home_sums():
        red_y[y] = sum_x[...]
        for d in range(1, NY):
            k = (y + d) % NY
            share_copy(sum_x, red_y, k, K_Y + k, other_core).wait_recv()
        sum_y[...] = total_of(red_y, NY)
        reduce_over(sum_y, sum_z, red_z, NZ, z, lambda i: dev(x, y, i, c), K_Z)
        for d in range(1, NY):
            spread_copy((y + d) % NY).start()

    with jax.named_scope("text_load"):
        loads[TXT].wait()
        normalize(TXT)
    with jax.named_scope("greeting"):
        pl.semaphore_wait(barrier, n_greet)
    with jax.named_scope("sends"):
        send_legs(TXT)
        loads[IMG].wait()
        normalize(IMG)
        send_plain(TXT)
        send_legs(IMG)

    phase = (z // 2) % 3
    after = dev(x, y, (z + 2) % NZ, c)

    def take_turn(kind):
        def await_turn():
            pl.semaphore_wait(turn_sem, 1)

        def pass_turn():
            pl.semaphore_signal(turn_sem, inc=1, device_id=after, device_id_type=MESH)

        @pl.when(on_seam | is_relay)
        def _():
            if kind == TXT:
                pl.when(phase > 0)(await_turn)
            else:
                await_turn()

        @pl.when(on_seam)
        def _():
            for j in range(DIRECT):
                seam_send(kind, j).start()
            seam_send(kind, 0).wait_send()

        @pl.when(is_relay)
        def _():
            for j in range(DIRECT, CHUNKS):
                arrived(RELAY, kind, j)
                relay_copy(kind, j).start()
            relay_copy(kind, DIRECT).wait_send()

        @pl.when(on_seam | is_relay)
        def _():
            if kind == TXT:
                pass_turn()
            else:
                pl.when(phase < 2)(pass_turn)

    pl.when(phase == 0)(lambda: take_turn(TXT))
    with jax.named_scope("own_pair"):
        pair(OWN, TXT, True)
    pl.when(phase > 0)(lambda: take_turn(TXT))
    pair(OWN, IMG, True)

    crossing = (at_top & (c == 0)) | (at_bottom & (c == 1))

    def others(kind):
        def rest():
            await_block(rest_slot, kind)
            pair(rest_slot, kind, False)

        await_block(SIB, kind)
        pair(SIB, kind, False)
        if kind == IMG:
            pl.when(crossing)(rest)
        pass_on(kind)
        pair(from_slot, kind, False)
        if kind == IMG:
            pl.when(jnp.logical_not(crossing))(rest)
        else:
            rest()
        await_block(FWD, kind)
        pair(FWD, kind, False)

    others(TXT)
    early = is_relay & (phase < 1)
    pl.when(early)(lambda: take_turn(IMG))
    reduce_over(part, sum_c, red_c, 2, c, lambda i: dev(x, y, z, i), K_C)
    reduce_over(sum_c, sum_x, red_x, NX, x, lambda i: dev(i, y, z, c), K_X)

    @pl.when(jnp.logical_not(at_home))
    def _():
        gather_copy().start()

    send_plain(IMG)
    pl.when(jnp.logical_not(early))(lambda: take_turn(IMG))

    finish(IMG)
    others(IMG)

    @pl.when(at_home)
    def _():
        home_sums()

    with jax.named_scope("finish_text"):
        finish(TXT)

    scaled = 1.0 / (rows * NX * NY * NZ * 2)

    @pl.when(at_home)
    def _():
        scale_out[0] = jnp.sum(sum_z[...]) * scaled
        for d in range(1, NY):
            spread_copy((y + d) % NY).wait_send()

    @pl.when(jnp.logical_not(at_home))
    def _():
        spread_copy(y).wait_recv()
        scale_out[0] = jnp.sum(red_b[0]) * scaled
        gather_copy().wait_send()

    with jax.named_scope("sent"):
        def sent(n, kind, j):
            remote(OWN, SIB, kind, j, send_sem.at[n, kind, j], other_core).wait_send()

        for kind in (TXT, IMG):
            for j in range(CHUNKS):
                sent(1, kind, j)
                sent(2, kind, j)
                remote(from_slot, FWD, kind, j, fwd_sem.at[kind, j], other_core).wait_send()
                if j == 0:
                    pl.when(jnp.logical_not(on_seam))(lambda: sent(0, kind, 0))
                else:
                    sent(0, kind, j)

        @pl.when(is_relay)
        def _():
            for kind in (TXT, IMG):
                for j in range(DIRECT + 1, CHUNKS):
                    relay_copy(kind, j).wait_send()

    for kind in (IMG, TXT):
        for h in range(2):
            at = pl.ds(h * half, half)
            out = (image_out, text_out)[kind]
            pltpu.make_async_copy(acc.at[kind, at], out.at[at], out_sem.at[kind, h]).wait()


def local(image_embed, text_embed, logit_scale, logit_bias):
    rows, width = image_embed.shape
    whole = jax.ShapeDtypeStruct((rows, width), jnp.float32)
    n_red = 2 + NX + 2 * NY + NZ
    return pl.pallas_call(
        kernel,
        name="window_loss",
        out_shape=(whole, whole, jax.ShapeDtypeStruct((1,), jnp.float32)),
        in_specs=[
            pl.BlockSpec(memory_space=pltpu.SMEM),
            pl.BlockSpec(memory_space=pltpu.SMEM),
            pl.BlockSpec(memory_space=pl.ANY),
            pl.BlockSpec(memory_space=pl.ANY),
        ],
        out_specs=(
            pl.BlockSpec(memory_space=pl.ANY),
            pl.BlockSpec(memory_space=pl.ANY),
            pl.BlockSpec(memory_space=pltpu.SMEM),
        ),
        scratch_shapes=[
            pltpu.VMEM((6, 2, rows, width), jnp.bfloat16),
            pltpu.VMEM((2, rows, width), jnp.float32),
            pltpu.VMEM((2, rows, 128), jnp.float32),
            pltpu.VMEM((2, rows, width), jnp.float32),
            *[pltpu.VMEM((8, 128), jnp.float32)] * 5,
            pltpu.VMEM((2, 8, 128), jnp.float32),
            pltpu.VMEM((NY, 8, 128), jnp.float32),
            pltpu.VMEM((NZ, 8, 128), jnp.float32),
            pltpu.VMEM((NX, 8, 128), jnp.float32),
            pltpu.VMEM((1, 8, 128), jnp.float32),
            pltpu.SemaphoreType.DMA((2,)),
            pltpu.SemaphoreType.DMA((2, 2)),
            pltpu.SemaphoreType.DMA((3, 2, CHUNKS)),
            pltpu.SemaphoreType.DMA((2, CHUNKS)),
            pltpu.SemaphoreType.DMA((2, CHUNKS)),
            pltpu.SemaphoreType.DMA((5, 2, CHUNKS)),
            pltpu.SemaphoreType.DMA((n_red,)),
            pltpu.SemaphoreType.DMA((n_red,)),
            pltpu.SemaphoreType.REGULAR,
        ],
        compiler_params=pltpu.CompilerParams(
            collective_id=0, has_side_effects=True, vmem_limit_bytes=60 * 2**20
        ),
        cost_estimate=pl.CostEstimate(
            flops=20 * 2 * rows * rows * width,
            bytes_accessed=4 * 4 * rows * width,
            transcendentals=10 * rows * rows,
        ),
    )(logit_scale, logit_bias, image_embed, text_embed)


def solution(mesh):
    placed = (P(("blk", "group"), None), P(("blk", "group"), None), P(), P())
    return jax.shard_map(
        local,
        mesh=mesh,
        in_specs=placed,
        out_specs=(P(("blk", "group"), None), P(("blk", "group"), None), P()),
        check_vma=False,
    )
```
